512 devices in a mesh: mem: 16 (over x, z_lo), tile: 32 (over y, z_hi, core).
Axes of the slice: x: 4, y: 4, z: 16 (z_hi: 4, z_lo: 4; z = z_hi * 4 + z_lo), core: 2. Of those that a mesh axis runs over, the one named last changes fastest.
Arguments:
- controls: float32 [128, 512, 1792], P('mem', 'tile'), may hold values from -6 to 6
- perturbations: bfloat16 [128, 4, 512, 1792], P('mem', None, 'tile'), may hold values from -1.5 to 1.5
- jacobian: float32 [4, 512, 1792], P(None, 'tile'), may hold values from -3 to 3
- obs_weight: float32 [512, 1792], P('tile'), may hold values from 0.5 to 4
- radar_mask: int32 [512, 1792], P('tile'), may hold values 0 or 1
- row_faces: float32 [512, 1792], P('tile'), may hold values from 0.12 to 0.25
- col_faces: float32 [512, 1792], P('tile'), may hold values from 0.12 to 0.25
Outputs:
- gradient: float32 [128, 512, 1792], P('mem', 'tile')
The draws below stay inside these ranges and needn't reach their ends.
All inputs are finite; a program needn't handle non-finite values. No bound on the sum of `radar_mask` on one device may be relied on, other than what follows from the above.
Results may differ from the reference program's by a relative error of at most 0.0003.
Values sent between devices are 32-bit elements; how exact they have to be, the bound alone decides.
A program may use at most 64 MiB of HBM per device.

```python
import math
import jax
import jax.numpy as jnp
from jax import lax

MEMBERS = 128
VARS = 4
COLS = 1792
STEPS = 4
ROWS = 512


def with_ends(drawn, rng, low, largest):
    longest = drawn.shape.index(max(drawn.shape))
    spots = []
    for shift in (0, 1):
        where = [jax.random.randint(jax.random.fold_in(rng, axis), (), 0, length) for axis, length in enumerate(drawn.shape)]
        where[longest] = (where[longest] + shift) % drawn.shape[longest]
        spots.append(tuple(where))
    return drawn.at[spots[0]].set(low).at[spots[1]].set(largest)


def block_scale(stream_key, extent, shards, low, largest):
    loudness, own = 1.0, jax.random.fold_in(stream_key, 6)
    for position, shards_of in shards:
        heights = jnp.exp(jax.random.uniform(jax.random.fold_in(own, position), (shards_of,), jnp.float32, low / len(shards), largest / len(shards)))
        loudness = loudness * jnp.repeat(heights, extent[position] // shards_of).reshape([-1 if axis == position else 1 for axis in range(len(extent))])
    return loudness


def bell_draw(stream_key, extent, scale, bound, shards=(), dtype=jnp.bfloat16):
    result = scale * jax.random.normal(stream_key, extent, jnp.float32)
    if shards:
        result = result * block_scale(stream_key, extent, shards, -0.22, 0.18)
    return jnp.clip(result, -bound, bound).astype(dtype)


def setup_inputs(seed: int = 0) -> dict:
    key_of = jax.random.split(jax.random.key(seed), 8)
    return {
        "controls": bell_draw(key_of[0], (MEMBERS, ROWS, COLS), 1.0, 6.0, ((0, 16), (1, 32)), jnp.float32),
        "perturbations": bell_draw(key_of[1], (MEMBERS, VARS, ROWS, COLS), 0.25, 1.5, ((0, 16), (2, 32))),
        "jacobian": bell_draw(key_of[2], (VARS, ROWS, COLS), 0.5, 3.0, ((1, 32),), jnp.float32),
        "obs_weight": jnp.clip(jnp.exp(math.log(4.0) - 2.0794415 * jax.random.uniform(key_of[3], (ROWS, COLS), jnp.float32) ** block_scale(key_of[3], (ROWS, COLS), ((0, 32),), -0.2, 0.2)), 0.5, 4.0),
        "radar_mask": with_ends((jax.random.randint(key_of[4], (ROWS, COLS), 0, 2) < 1).astype(jnp.int32), jax.random.fold_in(key_of[4], 1), 0, 1),
        "row_faces": jnp.clip(0.12 + 0.13 * jax.random.uniform(key_of[5], (ROWS, COLS), jnp.float32) ** block_scale(key_of[5], (ROWS, COLS), ((0, 32),), -0.2, 0.2), 0.12, 0.25),
        "col_faces": jnp.clip(0.12 + 0.13 * jax.random.uniform(key_of[6], (ROWS, COLS), jnp.float32) ** block_scale(key_of[6], (ROWS, COLS), ((0, 32),), -0.2, 0.2), 0.12, 0.25),
    }


def diffuse(values, row_coef, col_coef):
    row_flux = row_coef[..., :-1, :] * (values[..., 1:, :] - values[..., :-1, :])
    col_flux = col_coef[..., :, :-1] * (values[..., :, 1:] - values[..., :, :-1])
    zeros_row = jnp.zeros_like(values[..., :1, :])
    zeros_col = jnp.zeros_like(values[..., :, :1])
    values = values + jnp.concatenate([row_flux, zeros_row], -2) - jnp.concatenate([zeros_row, row_flux], -2)
    return values + jnp.concatenate([col_flux, zeros_col], -1) - jnp.concatenate([zeros_col, col_flux], -1)


def reference(controls, perturbations, jacobian, obs_weight, radar_mask, row_faces, col_faces):
    row_index = lax.broadcasted_iota(jnp.int32, row_faces.shape, 0)
    row_coef = jnp.where(row_index < row_faces.shape[0] - 1, row_faces, jnp.zeros_like(row_faces))
    col_coef = col_faces

    def localize(field):
        for repeat in range(STEPS):
            field = diffuse(field, row_coef, col_coef)
        return field

    def accumulate(carry, member):
        control, spread = member
        localized = localize(control)
        return carry + spread.astype(jnp.float32) * localized[None], None

    increment, _ = lax.scan(accumulate, jnp.zeros(jacobian.shape, jnp.float32), (controls, perturbations))
    reflect = jnp.sum(jacobian * increment, 0)
    weighted = radar_mask.astype(jnp.float32) * obs_weight * reflect
    adjoint_inc = jacobian * weighted[None]

    def backward(member):
        control, spread = member
        sensitivity = jnp.sum(spread.astype(jnp.float32) * adjoint_inc, 0)
        return control + localize(sensitivity)

    return lax.map(backward, (controls, perturbations))
```

```python
import jax
import jax.numpy as jnp
from jax import lax
from jax.experimental import pallas as pl
from jax.experimental.pallas import tpu as pltpu
from jax.sharding import PartitionSpec as P

MEM = 16
TILE = 32
H = 4
MESH = pl.DeviceIdType.MESH
f32 = jnp.float32


def kernel(ctl, pert, jac, obs, msk, rf, cf, out,
           C, A, B, Q, K, KR, KC, Pv, Jv, nat, natm, part, recv, rown, R, Rup, Rdn, O,
           lsem, csem, osem, hs, hr, ss, sr):
    G = Q.shape[1]
    n = Q.shape[2]
    E = Q.shape[0]
    rows = E - 2 * H
    m = lax.axis_index("mem")
    t = lax.axis_index("tile")
    x = m // 4
    z = m % 4
    has_up = t > 0
    has_dn = t < TILE - 1

    bar = pltpu.get_barrier_semaphore()

    def greet(mm, tt):
        pl.semaphore_signal(bar, inc=1, device_id=(mm, tt), device_id_type=MESH)

    def ring(i, carry):
        greet((m + i) % MEM, t)
        return carry

    def side(tt, full_z, own_z):
        @pl.when(z == full_z)
        def _():
            def body(i, carry):
                greet(i, tt)
                return carry
            lax.fori_loop(0, MEM, body, 0)

        @pl.when(z != full_z)
        def _():
            def body(i, carry):
                greet(i * 4 + own_z, tt)
                return carry
            lax.fori_loop(0, 4, body, 0)

            @pl.when(z != own_z)
            def _():
                greet(m, tt)

    lax.fori_loop(1, MEM, ring, 0)

    @pl.when(has_up)
    def _():
        side(t - 1, 0, 3)

    @pl.when(has_dn)
    def _():
        side(t + 1, 3, 0)

    loads = [
        pltpu.make_async_copy(pert, Pv, lsem.at[0]),
        pltpu.make_async_copy(jac, Jv, lsem.at[1]),
        pltpu.make_async_copy(rf, nat.at[0], lsem.at[2]),
        pltpu.make_async_copy(cf, nat.at[1], lsem.at[3]),
        pltpu.make_async_copy(obs, nat.at[2], lsem.at[4]),
        pltpu.make_async_copy(msk, natm, lsem.at[5]),
    ]
    for cp in loads:
        cp.start()

    def cload(r):
        return pltpu.make_async_copy(ctl.at[:, r, :], C.at[1 + H + r], csem.at[r])

    for r in range(rows):
        cload(r).start()

    zero = jnp.zeros((G, n), f32)
    for e in list(range(0, H + 1)) + list(range(H + rows + 1, E + 2)):
        C[e] = zero
        A[e] = zero
        B[e] = zero
    for e in (0, E + 1):
        KR[e] = zero
        KC[e] = zero
    line = jnp.zeros((1, n), f32)

    @pl.when(jnp.logical_not(has_up))
    def _():
        for e in range(H):
            Q[e] = zero
            for i in range(3):
                K[i, e] = line
        for e in range(2 * H):
            Rup[e] = line

    @pl.when(jnp.logical_not(has_dn))
    def _():
        for e in range(H + rows, E):
            Q[e] = zero
            for i in range(3):
                K[i, e] = line
        for e in range(2 * H):
            Rdn[e] = line

    for cp in loads[2:]:
        cp.wait()
    last = jnp.where(has_dn, 1.0, 0.0).astype(f32)
    lane = lax.broadcasted_iota(jnp.int32, (1, n), 1)
    for r in range(rows):
        row = nat[0, r:r + 1, :]
        K[0, H + r] = row * last if r == rows - 1 else row
        K[1, H + r] = jnp.where(lane < n - 1, nat[1, r:r + 1, :], 0.0)
        K[2, H + r] = nat[2, r:r + 1, :] * natm[r:r + 1, :].astype(f32)

    loads[0].wait()
    loads[1].wait()

    def qtile(j, carry):
        cols = pl.ds(pl.multiple_of(j * 128, 128), 128)
        q = Pv[:, 0, :, cols].astype(f32) * Jv[0, :, cols][None]
        for v in range(1, 4):
            q = q + Pv[:, v, :, cols].astype(f32) * Jv[v, :, cols][None]
        Q[H:H + rows, :, cols] = jnp.swapaxes(q, 0, 1)
        return carry

    lax.fori_loop(0, n // 128, qtile, 0)

    near = jnp.where(z == 0, 16, jnp.where(z == 3, 4, 5))
    far = jnp.where(z == 3, 16, jnp.where(z == 0, 4, 5))
    pl.semaphore_wait(bar, MEM - 1 + jnp.where(has_up, near, 0) + jnp.where(has_dn, far, 0))

    def halo(buf, up, i):
        if buf is K:
            src = K.at[:, pl.ds(H if up else rows, H)]
            dst = K.at[:, pl.ds(H + rows if up else 0, H)]
        else:
            src = Q.at[pl.ds(H if up else rows, H)]
            dst = Q.at[pl.ds(H + rows if up else 0, H)]
        return pltpu.make_async_remote_copy(
            src, dst, hs.at[i], hr.at[i], device_id=(m, t - 1 if up else t + 1), device_id_type=MESH)

    @pl.when(has_up)
    def _():
        halo(K, True, 0).start()
        halo(Q, True, 2).start()

    @pl.when(has_dn)
    def _():
        halo(K, False, 1).start()
        halo(Q, False, 3).start()

    def widen(e, carry):
        KR[1 + e] = jnp.broadcast_to(K[0, e], (G, n))
        KC[1 + e] = jnp.broadcast_to(K[1, e], (G, n))
        return carry

    lax.fori_loop(H, H + rows, widen, 0)
    for r in range(rows):
        cload(r).wait()

    @pl.when(has_up)
    def _():
        halo(K, False, 1).wait_recv()

    @pl.when(has_dn)
    def _():
        halo(K, True, 0).wait_recv()

    lax.fori_loop(0, H, widen, 0)
    lax.fori_loop(H + rows, E, widen, 0)

    def stencil(src, e):
        v = src[1 + e]
        down = KR[1 + e] * (src[2 + e] - v)
        up = KR[e] * (v - src[e])
        flux = KC[1 + e] * (pltpu.roll(v, n - 1, 1) - v)
        return v + (down - up) + (flux - pltpu.roll(flux, 1, 1))

    def step(src, dst, lo, hi):
        def body(e, carry):
            dst[1 + e] = stencil(src, e)
            return carry
        lax.fori_loop(lo, hi, body, 0)

    step(C, A, H - 1, H + rows + 1)
    step(A, B, H - 2, H + rows + 2)
    step(B, A, H - 3, H + rows + 3)
    step(A, B, 0, E)

    def product(e, carry):
        part[e] = jnp.sum(B[1 + e] * Q[e], axis=0, keepdims=True)
        return carry

    lax.fori_loop(H, H + rows, product, 0)

    @pl.when(has_up)
    def _():
        halo(Q, False, 3).wait_recv()

    @pl.when(has_dn)
    def _():
        halo(Q, True, 2).wait_recv()

    lax.fori_loop(0, H, product, 0)
    lax.fori_loop(H + rows, E, product, 0)

    def owned(zz, xx):
        return ((2 * xx, 2), (8 + xx, 1), (12 + xx, 1), (16 + 2 * xx, 2))[zz]

    def scatter(i, carry):
        xx = (x + i) % 4
        for zz in range(4):
            start, count = owned(zz, xx)

            @pl.when(jnp.logical_or(xx != x, z != zz))
            def _():
                pltpu.make_async_remote_copy(
                    part.at[pl.ds(start, count)], recv.at[m, pl.ds(0, count)], ss.at[0], sr.at[0],
                    device_id=(xx * 4 + zz, t), device_id_type=MESH).start()
        return carry

    lax.fori_loop(0, 4, scatter, 0)

    peer = (m + 1) % MEM

    def waiter(ref, sems):
        return pltpu.make_async_remote_copy(ref, ref, sems[0], sems[1], device_id=(peer, t), device_id_type=MESH)

    rs = (ss.at[0], sr.at[0])
    ag = (ss.at[1], sr.at[1])
    nu = (ss.at[2], sr.at[2])
    nd = (ss.at[3], sr.at[3])
    for zz in range(4):
        start, count = owned(zz, x)

        @pl.when(z == zz)
        def _():
            recv[m, 0:count] = part[pl.ds(start, count)]
            waiter(recv.at[pl.ds(0, MEM - 1), pl.ds(0, count)], rs).wait_recv()
            total = recv[0, 0:count]
            for i in range(1, MEM):
                total = total + recv[i, 0:count]
            rown[0:count] = total
            R[pl.ds(start, count)] = total

            def gather(i, carry):
                pltpu.make_async_remote_copy(
                    rown.at[pl.ds(0, count)], R.at[pl.ds(start, count)], ag[0], ag[1],
                    device_id=((m + i) % MEM, t), device_id_type=MESH).start()
                return carry

            if zz in (0, 3):
                near = has_up if zz == 0 else has_dn
                sem = nu if zz == 0 else nd
                dst = Rdn if zz == 0 else Rup

                @pl.when(near)
                def _():
                    def cross(i, carry):
                        pltpu.make_async_remote_copy(
                            rown.at[pl.ds(0, 2)], dst.at[pl.ds(2 * x, 2)], sem[0], sem[1],
                            device_id=((m + i) % MEM, t - 1 if zz == 0 else t + 1), device_id_type=MESH).start()
                        return carry
                    lax.fori_loop(0, MEM, cross, 0)

            lax.fori_loop(1, MEM, gather, 0)
            waiter(R.at[pl.ds(0, E - count)], ag).wait_recv()

    @pl.when(has_up)
    def _():
        waiter(Rup, nd).wait_recv()

    @pl.when(has_dn)
    def _():
        waiter(Rdn, nu).wait_recv()

    def spread(e, extra):
        r = R[e]
        if extra is not None:
            r = r + extra
        A[1 + e] = Q[e] * jnp.broadcast_to(K[2, e] * r, (G, n))

    def spread_up(e, carry):
        spread(e, Rup[e])
        return carry

    def spread_mid(e, carry):
        spread(e, None)
        return carry

    def spread_dn(e, carry):
        spread(e, Rdn[e - rows])
        return carry

    lax.fori_loop(0, 2 * H, spread_up, 0)
    lax.fori_loop(2 * H, rows, spread_mid, 0)
    lax.fori_loop(rows, E, spread_dn, 0)
    step(A, B, 1, E - 1)
    step(B, A, 2, E - 2)
    step(A, B, 3, E - 3)

    def store(r):
        return pltpu.make_async_copy(O.at[r], out.at[:, r, :], osem.at[r])

    def final(r, carry):
        O[r] = C[1 + H + r] + stencil(B, H + r)
        return carry

    for r in range(rows):
        final(r, 0)
        store(r).start()

    @pl.when(has_up)
    def _():
        halo(K, True, 0).wait_send()
        halo(Q, True, 2).wait_send()

    @pl.when(has_dn)
    def _():
        halo(K, False, 1).wait_send()
        halo(Q, False, 3).wait_send()

    for zz in range(4):
        count = owned(zz, 0)[1]

        @pl.when(z == zz)
        def _():
            waiter(part.at[pl.ds(0, E - count)], rs).wait_send()
            waiter(recv.at[pl.ds(0, MEM - 1), pl.ds(0, count)], ag).wait_send()
            if zz in (0, 3):
                @pl.when(has_up if zz == 0 else has_dn)
                def _():
                    waiter(recv, nu if zz == 0 else nd).wait_send()

    for r in range(rows):
        store(r).wait()


def per_device(controls, perturbations, jacobian, obs_weight, radar_mask, row_faces, col_faces):
    G, rows, n = controls.shape
    E = rows + 2 * H
    big = pltpu.VMEM((E + 2, G, n), f32)
    row = lambda *s: pltpu.VMEM(s + (1, n), f32)
    dma = pltpu.SemaphoreType.DMA
    return pl.pallas_call(
        kernel,
        out_shape=jax.ShapeDtypeStruct(controls.shape, f32),
        in_specs=[pl.BlockSpec(memory_space=pl.ANY)] * 7,
        out_specs=pl.BlockSpec(memory_space=pl.ANY),
        scratch_shapes=[
            big, big, big, pltpu.VMEM((E, G, n), f32), row(3, E), big, big,
            pltpu.VMEM(perturbations.shape, jnp.bfloat16), pltpu.VMEM(jacobian.shape, f32),
            pltpu.VMEM((3, rows, n), f32), pltpu.VMEM((rows, n), jnp.int32),
            row(E), row(MEM, 2), row(2), row(E), row(2 * H), row(2 * H),
            pltpu.VMEM((rows, G, n), f32),
            dma((6,)), dma((rows,)), dma((rows,)), dma((4,)), dma((4,)), dma((4,)), dma((4,)),
        ],
        compiler_params=pltpu.CompilerParams(
            collective_id=0, has_side_effects=True, vmem_limit_bytes=40 * 1024 * 1024),
    )(controls, perturbations, jacobian, obs_weight, radar_mask, row_faces, col_faces)


def solution(mesh):
    placed = (
        P("mem", "tile", None),
        P("mem", None, "tile", None),
        P(None, "tile", None),
        P("tile", None),
        P("tile", None),
        P("tile", None),
        P("tile", None),
    )
    return jax.shard_map(
        per_device, mesh=mesh, in_specs=placed, out_specs=P("mem", "tile", None), check_vma=False
    )
```

```python
import jax
import jax.numpy as jnp
from jax import lax
from jax.experimental import pallas as pl
from jax.experimental.pallas import tpu as pltpu
from jax.sharding import PartitionSpec as P

MEM = 16
TILE = 32
H = 4
MESH = pl.DeviceIdType.MESH
f32 = jnp.float32
UA, UB, UC, UD, UE = 9, 5, 11, 8, 8


def kernel(ctl, pert, jac, obs, msk, rf, cf, out,
           C, A, B, Q, K, KR, KC, KL, Pv, Jv, nat, natm, part, recv, rown, R, Rup, Rdn, O,
           lsem, psem, csem, osem, hs, hr, fs, fr, ss, sr):
    G = Q.shape[1]
    n = Q.shape[2]
    E = Q.shape[0]
    rows = E - 2 * H
    m = lax.axis_index("mem")
    t = lax.axis_index("tile")
    x = m // 4
    z = m % 4
    has_up = t > 0
    has_dn = t < TILE - 1

    bar = pltpu.get_barrier_semaphore()

    def greet(mm, tt):
        pl.semaphore_signal(bar, inc=1, device_id=(mm, tt), device_id_type=MESH)

    def ring(i, carry):
        greet((m + i) % MEM, t)
        return carry

    def side(tt, full_z, own_z):
        @pl.when(z == full_z)
        def _():
            def body(i, carry):
                greet(i, tt)
                return carry
            lax.fori_loop(0, MEM, body, 0)

        @pl.when(z != full_z)
        def _():
            def body(i, carry):
                greet(i * 4 + own_z, tt)
                return carry
            lax.fori_loop(0, 4, body, 0)

            @pl.when(z != own_z)
            def _():
                greet(m, tt)

    step_cols = 256
    parts = n // step_cols
    small = [
        pltpu.make_async_copy(rf, nat.at[0], lsem.at[0]),
        pltpu.make_async_copy(cf, nat.at[1], lsem.at[1]),
        pltpu.make_async_copy(obs, nat.at[2], lsem.at[2]),
        pltpu.make_async_copy(msk, natm, lsem.at[3]),
    ]
    jload = pltpu.make_async_copy(jac, Jv, lsem.at[4])

    def pload(i):
        cols = pl.ds(i * step_cols, step_cols)
        return pltpu.make_async_copy(pert.at[:, :, :, cols], Pv.at[:, :, :, cols], psem.at[i])

    def cload(r):
        return pltpu.make_async_copy(ctl.at[:, r, :], C.at[1 + H + r], csem.at[r])

    jload.start()
    for i in range(parts):
        pload(i).start()
    for cp in small:
        cp.start()

    lax.fori_loop(1, MEM, ring, 0)

    @pl.when(has_up)
    def _():
        side(t - 1, 0, 3)

    @pl.when(has_dn)
    def _():
        side(t + 1, 3, 0)

    line = jnp.zeros((1, n), f32)

    @pl.when(jnp.logical_not(has_up))
    def _():
        for e in range(H):
            Q[e] = jnp.zeros((G, n), f32)
            for i in range(3):
                K[i, e] = line
        for e in range(2 * H):
            Rup[e] = line

    @pl.when(jnp.logical_not(has_dn))
    def _():
        for e in range(H + rows, E):
            Q[e] = jnp.zeros((G, n), f32)
            for i in range(3):
                K[i, e] = line
        for e in range(2 * H):
            Rdn[e] = line

    for cp in small:
        cp.wait()
    last = jnp.where(has_dn, 1.0, 0.0).astype(f32)
    lane = lax.broadcasted_iota(jnp.int32, (1, n), 1)
    for r in range(rows):
        row = nat[0, r:r + 1, :]
        K[0, H + r] = row * last if r == rows - 1 else row
        K[1, H + r] = jnp.where(lane < n - 1, nat[1, r:r + 1, :], 0.0)
        K[2, H + r] = nat[2, r:r + 1, :] * natm[r:r + 1, :].astype(f32)

    def qtile(j, carry):
        cols = pl.ds(pl.multiple_of(j * 128, 128), 128)
        q = Pv[:, 0, :, cols].astype(f32) * Jv[0, :, cols][None]
        for v in range(1, 4):
            q = q + Pv[:, v, :, cols].astype(f32) * Jv[v, :, cols][None]
        Q[H:H + rows, :, cols] = jnp.swapaxes(q, 0, 1)
        return carry

    jload.wait()
    for i in range(parts):
        pload(i).wait()
        lax.fori_loop(i * step_cols // 128, (i + 1) * step_cols // 128, qtile, 0)
    for r in range(rows):
        cload(r).start()

    near = jnp.where(z == 0, 16, jnp.where(z == 3, 4, 5))
    far = jnp.where(z == 3, 16, jnp.where(z == 0, 4, 5))
    pl.semaphore_wait(bar, MEM - 1 + jnp.where(has_up, near, 0) + jnp.where(has_dn, far, 0))

    def near_copy(src, dst, up, i):
        return pltpu.make_async_remote_copy(
            src, dst, hs.at[i], hr.at[i], device_id=(m, t - 1 if up else t + 1), device_id_type=MESH)

    def halo(up):
        return near_copy(
            Q.at[pl.ds(H if up else rows, H)], Q.at[pl.ds(H + rows if up else 0, H)], up, 2 if up else 3)

    def piece(up):
        return near_copy(
            K.at[:, pl.ds((H if up else rows) + x, 1)], K.at[:, pl.ds((H + rows if up else 0) + x, 1)],
            up, 0 if up else 1)

    def hand_on(below, i):
        row = K.at[:, pl.ds((H + rows if below else 0) + x, 1)]
        k = 0 if below else 1
        return pltpu.make_async_remote_copy(
            row, row, fs.at[k], fr.at[k], device_id=(((x + i) % 4) * 4 + z, t), device_id_type=MESH)

    def handed(below):
        k = 0 if below else 1
        ref = K.at[:, pl.ds(0, 3)]
        return pltpu.make_async_remote_copy(
            ref, ref, fs.at[k], fr.at[k], device_id=(((x + 1) % 4) * 4 + z, t), device_id_type=MESH)

    @pl.when(has_up)
    def _():
        piece(True).start()

    @pl.when(has_dn)
    def _():
        piece(False).start()

    @pl.when(has_up)
    def _():
        halo(True).start()

    @pl.when(has_dn)
    def _():
        halo(False).start()

    zero = jnp.zeros((G, n), f32)
    for e in list(range(0, H + 1)) + list(range(H + rows + 1, E + 2)):
        C[e] = zero
        A[e] = zero
        B[e] = zero
    for e in (0, E + 1):
        KR[e] = zero
        KC[e] = zero
        KL[e] = zero
    def widen(e, carry):
        KR[1 + e] = jnp.broadcast_to(K[0, e], (G, n))
        KC[1 + e] = jnp.broadcast_to(K[1, e], (G, n))
        KL[1 + e] = jnp.broadcast_to(pltpu.roll(K[1, e], 1, 1), (G, n))
        return carry

    lax.fori_loop(H, H + rows, widen, 0)
    for r in range(rows):
        cload(r).wait()

    @pl.when(has_up)
    def _():
        piece(False).wait_recv()
        for i in range(1, 4):
            hand_on(False, i).start()

    @pl.when(has_dn)
    def _():
        piece(True).wait_recv()
        for i in range(1, 4):
            hand_on(True, i).start()

    @pl.when(has_up)
    def _():
        handed(False).wait_recv()

    @pl.when(has_dn)
    def _():
        handed(True).wait_recv()

    lax.fori_loop(0, H, widen, 0)
    lax.fori_loop(H + rows, E, widen, 0)

    def stencil(src, e, count):
        outs = []
        v = src[1 + e]
        up = KR[e] * (v - src[e])
        for i in range(count):
            nxt = src[2 + e + i]
            down = KR[1 + e + i] * (nxt - v)
            flux = KC[1 + e + i] * (pltpu.roll(v, n - 1, 1) - v)
            back = KL[1 + e + i] * (v - pltpu.roll(v, 1, 1))
            outs.append((v + (down - up)) + (flux - back))
            v, up = nxt, down
        return outs

    def step(src, dst, lo, hi, group):
        def body(i, carry):
            e = lo + i * group
            for k, o in enumerate(stencil(src, e, group)):
                dst[1 + e + k] = o
            return carry
        lax.fori_loop(0, (hi - lo) // group, body, 0)

    step(C, A, H - 1, H + rows + 1, UA)
    step(A, B, H - 2, H + rows + 2, UB)
    step(B, A, H - 3, H + rows + 3, UC)
    step(A, B, 0, E, UD)

    def product(e, carry):
        part[e] = jnp.sum(B[1 + e] * Q[e], axis=0, keepdims=True)
        return carry

    lax.fori_loop(H, H + rows, product, 0)

    @pl.when(has_up)
    def _():
        halo(False).wait_recv()

    @pl.when(has_dn)
    def _():
        halo(True).wait_recv()

    lax.fori_loop(0, H, product, 0)
    lax.fori_loop(H + rows, E, product, 0)

    def owned(zz, xx):
        return ((2 * xx, 2), (8 + xx, 1), (12 + xx, 1), (16 + 2 * xx, 2))[zz]

    def scatter(i, carry):
        xx = (x + i) % 4
        for zz in range(4):
            start, count = owned(zz, xx)

            @pl.when(jnp.logical_or(xx != x, z != zz))
            def _():
                pltpu.make_async_remote_copy(
                    part.at[pl.ds(start, count)], recv.at[m, pl.ds(0, count)], ss.at[0], sr.at[0],
                    device_id=(xx * 4 + zz, t), device_id_type=MESH).start()
        return carry

    lax.fori_loop(0, 4, scatter, 0)

    peer = (m + 1) % MEM

    def waiter(ref, sems):
        return pltpu.make_async_remote_copy(ref, ref, sems[0], sems[1], device_id=(peer, t), device_id_type=MESH)

    rs = (ss.at[0], sr.at[0])
    ag = (ss.at[1], sr.at[1])
    nu = (ss.at[2], sr.at[2])
    nd = (ss.at[3], sr.at[3])
    for zz in range(4):
        start, count = owned(zz, x)

        @pl.when(z == zz)
        def _():
            recv[m, 0:count] = part[pl.ds(start, count)]
            waiter(recv.at[pl.ds(0, MEM - 1), pl.ds(0, count)], rs).wait_recv()
            total = recv[0, 0:count]
            for i in range(1, MEM):
                total = total + recv[i, 0:count]
            rown[0:count] = total
            R[pl.ds(start, count)] = total

            def gather(i, carry):
                pltpu.make_async_remote_copy(
                    rown.at[pl.ds(0, count)], R.at[pl.ds(start, count)], ag[0], ag[1],
                    device_id=((m + i) % MEM, t), device_id_type=MESH).start()
                return carry

            if zz in (0, 3):
                near = has_up if zz == 0 else has_dn
                sem = nu if zz == 0 else nd
                dst = Rdn if zz == 0 else Rup

                @pl.when(near)
                def _():
                    def cross(i, carry):
                        pltpu.make_async_remote_copy(
                            rown.at[pl.ds(0, 2)], dst.at[pl.ds(2 * x, 2)], sem[0], sem[1],
                            device_id=((m + i) % MEM, t - 1 if zz == 0 else t + 1), device_id_type=MESH).start()
                        return carry
                    lax.fori_loop(0, MEM, cross, 0)

            lax.fori_loop(1, MEM, gather, 0)
            waiter(R.at[pl.ds(0, E - count)], ag).wait_recv()

    @pl.when(has_up)
    def _():
        waiter(Rup, nd).wait_recv()

    @pl.when(has_dn)
    def _():
        waiter(Rdn, nu).wait_recv()

    def spread(e, extra):
        r = R[e]
        if extra is not None:
            r = r + extra
        A[1 + e] = Q[e] * jnp.broadcast_to(K[2, e] * r, (G, n))

    def spread_up(e, carry):
        spread(e, Rup[e])
        return carry

    def spread_mid(e, carry):
        spread(e, None)
        return carry

    def spread_dn(e, carry):
        spread(e, Rdn[e - rows])
        return carry

    lax.fori_loop(0, 2 * H, spread_up, 0)
    lax.fori_loop(2 * H, rows, spread_mid, 0)
    lax.fori_loop(rows, E, spread_dn, 0)
    step(A, B, 1, E - 1, UC)
    step(B, A, 2, E - 2, UB)
    step(A, B, 3, E - 3, UA)

    def store(r):
        return pltpu.make_async_copy(O.at[r], out.at[:, r, :], osem.at[r])

    for r in range(0, rows, UE):
        for k, o in enumerate(stencil(B, H + r, UE)):
            O[r + k] = C[1 + H + r + k] + o
            store(r + k).start()

    @pl.when(has_up)
    def _():
        piece(True).wait_send()
        halo(True).wait_send()
        handed(False).wait_send()

    @pl.when(has_dn)
    def _():
        piece(False).wait_send()
        halo(False).wait_send()
        handed(True).wait_send()

    for zz in range(4):
        count = owned(zz, 0)[1]

        @pl.when(z == zz)
        def _():
            waiter(part.at[pl.ds(0, E - count)], rs).wait_send()
            waiter(recv.at[pl.ds(0, MEM - 1), pl.ds(0, count)], ag).wait_send()
            if zz in (0, 3):
                @pl.when(has_up if zz == 0 else has_dn)
                def _():
                    waiter(recv, nu if zz == 0 else nd).wait_send()

    for r in range(rows):
        store(r).wait()


def per_device(controls, perturbations, jacobian, obs_weight, radar_mask, row_faces, col_faces):
    G, rows, n = controls.shape
    E = rows + 2 * H
    big = pltpu.VMEM((E + 2, G, n), f32)
    row = lambda *s: pltpu.VMEM(s + (1, n), f32)
    dma = pltpu.SemaphoreType.DMA
    return pl.pallas_call(
        kernel,
        out_shape=jax.ShapeDtypeStruct(controls.shape, f32),
        in_specs=[pl.BlockSpec(memory_space=pl.ANY)] * 7,
        out_specs=pl.BlockSpec(memory_space=pl.ANY),
        scratch_shapes=[
            big, big, big, pltpu.VMEM((E, G, n), f32), row(3, E), big, big, big,
            pltpu.VMEM(perturbations.shape, jnp.bfloat16), pltpu.VMEM(jacobian.shape, f32),
            pltpu.VMEM((3, rows, n), f32), pltpu.VMEM((rows, n), jnp.int32),
            row(E), row(MEM, 2), row(2), row(E), row(2 * H), row(2 * H),
            pltpu.VMEM((rows, G, n), f32),
            dma((5,)), dma((n // 256,)), dma((rows,)), dma((rows,)), dma((4,)), dma((4,)), dma((2,)), dma((2,)), dma((4,)), dma((4,)),
        ],
        compiler_params=pltpu.CompilerParams(
            collective_id=0, has_side_effects=True, vmem_limit_bytes=62 * 1024 * 1024),
    )(controls, perturbations, jacobian, obs_weight, radar_mask, row_faces, col_faces)


def solution(mesh):
    placed = (
        P("mem", "tile", None),
        P("mem", None, "tile", None),
        P(None, "tile", None),
        P("tile", None),
        P("tile", None),
        P("tile", None),
        P("tile", None),
    )
    return jax.shard_map(
        per_device, mesh=mesh, in_specs=placed, out_specs=P("mem", "tile", None), check_vma=False
    )
```

```python
import jax
import jax.numpy as jnp
from jax import lax
from jax.experimental import pallas as pl
from jax.experimental.pallas import tpu as pltpu
from jax.sharding import PartitionSpec as P

MEM = 16
TILE = 32
H = 4
MESH = pl.DeviceIdType.MESH
f32 = jnp.float32
UA, UB, UC, UD, UE = 9, 5, 11, 8, 8


def kernel(ctl, pert, jac, obs, msk, rf, cf, out,
           C, A, B, Q, K, KR, KC, KL, Pv, Jv, nat, natm, part, recv, rown, R, Rup, Rdn, O,
           lsem, psem, csem, osem, hs, hr, fs, fr, ss, sr):
    G = Q.shape[1]
    n = Q.shape[2]
    E = Q.shape[0]
    rows = E - 2 * H
    m = lax.axis_index("mem")
    t = lax.axis_index("tile")
    x = m // 4
    z = m % 4
    has_up = t > 0
    has_dn = t < TILE - 1

    bar = pltpu.get_barrier_semaphore()

    def greet(mm, tt):
        pl.semaphore_signal(bar, inc=1, device_id=(mm, tt), device_id_type=MESH)

    def ring(i, carry):
        greet((m + i) % MEM, t)
        return carry

    def side(tt, full_z, own_z):
        @pl.when(z == full_z)
        def _():
            def body(i, carry):
                greet(i, tt)
                return carry
            lax.fori_loop(0, MEM, body, 0)

        @pl.when(z != full_z)
        def _():
            def body(i, carry):
                greet(i * 4 + own_z, tt)
                return carry
            lax.fori_loop(0, 4, body, 0)

            @pl.when(z != own_z)
            def _():
                greet(m, tt)

    step_cols = 256
    parts = n // step_cols
    small = [
        pltpu.make_async_copy(rf, nat.at[0], lsem.at[0]),
        pltpu.make_async_copy(cf, nat.at[1], lsem.at[1]),
        pltpu.make_async_copy(obs, nat.at[2], lsem.at[2]),
        pltpu.make_async_copy(msk, natm, lsem.at[3]),
    ]
    jload = pltpu.make_async_copy(jac, Jv, lsem.at[4])

    def pload(i):
        cols = pl.ds(i * step_cols, step_cols)
        return pltpu.make_async_copy(pert.at[:, :, :, cols], Pv.at[:, :, :, cols], psem.at[i])

    def cload(r):
        return pltpu.make_async_copy(ctl.at[:, r, :], C.at[1 + H + r], csem.at[r])

    jload.start()
    for i in range(parts):
        pload(i).start()
    for cp in small:
        cp.start()

    lax.fori_loop(1, MEM, ring, 0)

    @pl.when(has_up)
    def _():
        side(t - 1, 0, 3)

    @pl.when(has_dn)
    def _():
        side(t + 1, 3, 0)

    line = jnp.zeros((1, n), f32)

    @pl.when(jnp.logical_not(has_up))
    def _():
        for e in range(H):
            Q[e] = jnp.zeros((G, n), f32)
            for i in range(3):
                K[i, e] = line
        for e in range(2 * H):
            Rup[e] = line

    @pl.when(jnp.logical_not(has_dn))
    def _():
        for e in range(H + rows, E):
            Q[e] = jnp.zeros((G, n), f32)
            for i in range(3):
                K[i, e] = line
        for e in range(2 * H):
            Rdn[e] = line

    for cp in small:
        cp.wait()
    last = jnp.where(has_dn, 1.0, 0.0).astype(f32)
    lane = lax.broadcasted_iota(jnp.int32, (1, n), 1)
    for r in range(rows):
        row = nat[0, r:r + 1, :]
        K[0, H + r] = row * last if r == rows - 1 else row
        K[1, H + r] = jnp.where(lane < n - 1, nat[1, r:r + 1, :], 0.0)
        K[2, H + r] = nat[2, r:r + 1, :] * natm[r:r + 1, :].astype(f32)

    def qtile(j, carry):
        cols = pl.ds(pl.multiple_of(j * 128, 128), 128)
        q = Pv[:, 0, :, cols].astype(f32) * Jv[0, :, cols][None]
        for v in range(1, 4):
            q = q + Pv[:, v, :, cols].astype(f32) * Jv[v, :, cols][None]
        Q[H:H + rows, :, cols] = jnp.swapaxes(q, 0, 1)
        return carry

    jload.wait()
    for i in range(parts):
        pload(i).wait()
        lax.fori_loop(i * step_cols // 128, (i + 1) * step_cols // 128, qtile, 0)
    for r in range(rows):
        cload(r).start()

    near = jnp.where(z == 0, 16, jnp.where(z == 3, 4, 5))
    far = jnp.where(z == 3, 16, jnp.where(z == 0, 4, 5))
    pl.semaphore_wait(bar, MEM - 1 + jnp.where(has_up, near, 0) + jnp.where(has_dn, far, 0))

    def near_copy(src, dst, up, i):
        return pltpu.make_async_remote_copy(
            src, dst, hs.at[i], hr.at[i], device_id=(m, t - 1 if up else t + 1), device_id_type=MESH)

    def halo(up, half):
        k = half * (H // 2)
        return near_copy(
            Q.at[pl.ds((H if up else rows) + k, H // 2)], Q.at[pl.ds((H + rows if up else 0) + k, H // 2)],
            up, (2 if up else 4) + half)

    def piece(up):
        return near_copy(
            K.at[:, pl.ds((H if up else rows) + x, 1)], K.at[:, pl.ds((H + rows if up else 0) + x, 1)],
            up, 0 if up else 1)

    def hand_on(below, i):
        row = K.at[:, pl.ds((H + rows if below else 0) + x, 1)]
        k = 0 if below else 1
        return pltpu.make_async_remote_copy(
            row, row, fs.at[k], fr.at[k], device_id=(((x + i) % 4) * 4 + z, t), device_id_type=MESH)

    def handed(below):
        k = 0 if below else 1
        ref = K.at[:, pl.ds(0, 3)]
        return pltpu.make_async_remote_copy(
            ref, ref, fs.at[k], fr.at[k], device_id=(((x + 1) % 4) * 4 + z, t), device_id_type=MESH)

    @pl.when(has_up)
    def _():
        piece(True).start()

    @pl.when(has_dn)
    def _():
        piece(False).start()

    def send_half(half):
        @pl.when(has_up)
        def _():
            halo(True, half).start()

        @pl.when(has_dn)
        def _():
            halo(False, half).start()

    send_half(0)

    zero = jnp.zeros((G, n), f32)
    for e in list(range(0, H + 1)) + list(range(H + rows + 1, E + 2)):
        C[e] = zero
        A[e] = zero
        B[e] = zero
    for e in (0, E + 1):
        KR[e] = zero
        KC[e] = zero
        KL[e] = zero
    def widen(e, carry):
        KR[1 + e] = jnp.broadcast_to(K[0, e], (G, n))
        KC[1 + e] = jnp.broadcast_to(K[1, e], (G, n))
        KL[1 + e] = jnp.broadcast_to(pltpu.roll(K[1, e], 1, 1), (G, n))
        return carry

    lax.fori_loop(H, H + rows, widen, 0)
    for r in range(rows):
        cload(r).wait()

    @pl.when(has_up)
    def _():
        piece(False).wait_recv()
        for i in range(1, 4):
            hand_on(False, i).start()

    @pl.when(has_dn)
    def _():
        piece(True).wait_recv()
        for i in range(1, 4):
            hand_on(True, i).start()

    send_half(1)

    @pl.when(has_up)
    def _():
        handed(False).wait_recv()

    @pl.when(has_dn)
    def _():
        handed(True).wait_recv()

    lax.fori_loop(0, H, widen, 0)
    lax.fori_loop(H + rows, E, widen, 0)

    def stencil(src, e, count):
        outs = []
        v = src[1 + e]
        up = KR[e] * (v - src[e])
        for i in range(count):
            nxt = src[2 + e + i]
            down = KR[1 + e + i] * (nxt - v)
            flux = KC[1 + e + i] * (pltpu.roll(v, n - 1, 1) - v)
            back = KL[1 + e + i] * (v - pltpu.roll(v, 1, 1))
            outs.append((v + (down - up)) + (flux - back))
            v, up = nxt, down
        return outs

    def step(src, dst, lo, hi, group):
        def body(i, carry):
            e = lo + i * group
            for k, o in enumerate(stencil(src, e, group)):
                dst[1 + e + k] = o
            return carry
        lax.fori_loop(0, (hi - lo) // group, body, 0)

    step(C, A, H - 1, H + rows + 1, UA)
    step(A, B, H - 2, H + rows + 2, UB)
    step(B, A, H - 3, H + rows + 3, UC)
    step(A, B, 0, E, UD)

    def product(e, carry):
        part[e] = jnp.sum(B[1 + e] * Q[e], axis=0, keepdims=True)
        return carry

    lax.fori_loop(H, H + rows, product, 0)

    peer = (m + 1) % MEM

    def to(src, dst, sem, mm, tt):
        return pltpu.make_async_remote_copy(
            src, dst, ss.at[sem], sr.at[sem], device_id=(mm, tt), device_id_type=MESH)

    def waiter(ref, sem):
        return to(ref, ref, sem, peer, t)

    mine = H + 4 * z + x
    late = jnp.where(z == 0, x, H + rows + x)
    owner_late = jnp.logical_or(z == 0, z == 3)

    def scatter(i, carry):
        o = (m + i) % MEM
        to(part.at[pl.ds(H + 4 * (o % 4) + o // 4, 1)], recv.at[0, pl.ds(m, 1)], 0, o, t).start()
        return carry

    lax.fori_loop(1, MEM, scatter, 0)

    @pl.when(has_up)
    def _():
        halo(False, 0).wait_recv()
        halo(False, 1).wait_recv()

    @pl.when(has_dn)
    def _():
        halo(True, 0).wait_recv()
        halo(True, 1).wait_recv()

    lax.fori_loop(0, H, product, 0)
    lax.fori_loop(H + rows, E, product, 0)

    def scatter_late(i, carry):
        xx = (x + 3 - i) % 4
        for zz, start in ((0, 0), (3, H + rows)):
            @pl.when(jnp.logical_or(xx != x, z != zz))
            def _():
                to(part.at[pl.ds(start + xx, 1)], recv.at[1, pl.ds(m, 1)], 1, xx * 4 + zz, t).start()
        return carry

    lax.fori_loop(0, 4, scatter_late, 0)

    def total(k, row):
        recv[k, pl.ds(m, 1)] = part[pl.ds(row, 1)]
        waiter(recv.at[k, pl.ds(0, MEM - 1)], k).wait_recv()
        sums = [recv[k, i:i + 1] for i in range(MEM)]
        while len(sums) > 1:
            sums = [a + b for a, b in zip(sums[::2], sums[1::2])]
        rown[k:k + 1] = sums[0]
        R[pl.ds(row, 1)] = sums[0]

    def gather(k, row):
        src = rown.at[pl.ds(k, 1)]

        def cross(i, carry, dst, at, sem, tt):
            to(src, dst.at[pl.ds(at, 1)], sem, (m + i) % MEM, tt).start()
            return carry

        @pl.when(jnp.logical_and(z == 0, has_up))
        def _():
            lax.fori_loop(0, MEM, lambda i, c: cross(i, c, Rdn, row, 4 + k, t - 1), 0)

        @pl.when(jnp.logical_and(z == 3, has_dn))
        def _():
            lax.fori_loop(0, MEM, lambda i, c: cross(i, c, Rup, row - rows, 6 + k, t + 1), 0)

        def own(i, carry):
            to(src, R.at[pl.ds(row, 1)], 2 + k, (m + i) % MEM, t).start()
            return carry

        lax.fori_loop(1, MEM, own, 0)

    total(0, mine)
    gather(0, mine)

    @pl.when(owner_late)
    def _():
        total(1, late)
        gather(1, late)

    waiter(R.at[pl.ds(0, MEM - 1)], 2).wait_recv()

    def spread(e, extra):
        r = R[e]
        if extra is not None:
            r = r + extra
        A[1 + e] = Q[e] * jnp.broadcast_to(K[2, e] * r, (G, n))

    def spread_up(e, carry):
        spread(e, Rup[e])
        return carry

    def spread_mid(e, carry):
        spread(e, None)
        return carry

    def spread_dn(e, carry):
        spread(e, Rdn[e - rows])
        return carry

    lax.fori_loop(2 * H, rows, spread_mid, 0)

    @pl.when(has_up)
    def _():
        waiter(Rup.at[pl.ds(0, H)], 6).wait_recv()

    @pl.when(has_dn)
    def _():
        waiter(Rdn.at[pl.ds(0, H)], 4).wait_recv()

    @pl.when(owner_late)
    def _():
        waiter(R.at[pl.ds(0, 2 * H - 1)], 3).wait_recv()

    @pl.when(jnp.logical_not(owner_late))
    def _():
        waiter(R.at[pl.ds(0, 2 * H)], 3).wait_recv()

    @pl.when(has_up)
    def _():
        waiter(Rup.at[pl.ds(0, H)], 7).wait_recv()

    @pl.when(has_dn)
    def _():
        waiter(Rdn.at[pl.ds(0, H)], 5).wait_recv()

    lax.fori_loop(0, 2 * H, spread_up, 0)
    lax.fori_loop(rows, E, spread_dn, 0)
    step(A, B, 1, E - 1, UC)
    step(B, A, 2, E - 2, UB)
    step(A, B, 3, E - 3, UA)

    def store(r):
        return pltpu.make_async_copy(O.at[r], out.at[:, r, :], osem.at[r])

    for r in range(0, rows, UE):
        for k, o in enumerate(stencil(B, H + r, UE)):
            O[r + k] = C[1 + H + r + k] + o
            store(r + k).start()

    @pl.when(has_up)
    def _():
        piece(True).wait_send()
        halo(True, 0).wait_send()
        halo(True, 1).wait_send()
        handed(False).wait_send()

    @pl.when(has_dn)
    def _():
        piece(False).wait_send()
        halo(False, 0).wait_send()
        halo(False, 1).wait_send()
        handed(True).wait_send()

    waiter(R.at[pl.ds(0, MEM - 1)], 0).wait_send()
    waiter(R.at[pl.ds(0, MEM - 1)], 2).wait_send()

    @pl.when(owner_late)
    def _():
        waiter(R.at[pl.ds(0, 2 * H - 1)], 1).wait_send()
        waiter(R.at[pl.ds(0, MEM - 1)], 3).wait_send()

    @pl.when(jnp.logical_not(owner_late))
    def _():
        waiter(R.at[pl.ds(0, 2 * H)], 1).wait_send()

    for zz, near, k in ((0, has_up, 4), (3, has_dn, 6)):
        @pl.when(jnp.logical_and(z == zz, near))
        def _():
            waiter(R.at[pl.ds(0, MEM)], k).wait_send()
            waiter(R.at[pl.ds(0, MEM)], k + 1).wait_send()

    for r in range(rows):
        store(r).wait()


def per_device(controls, perturbations, jacobian, obs_weight, radar_mask, row_faces, col_faces):
    G, rows, n = controls.shape
    E = rows + 2 * H
    big = pltpu.VMEM((E + 2, G, n), f32)
    row = lambda *s: pltpu.VMEM(s + (1, n), f32)
    dma = pltpu.SemaphoreType.DMA
    return pl.pallas_call(
        kernel,
        out_shape=jax.ShapeDtypeStruct(controls.shape, f32),
        in_specs=[pl.BlockSpec(memory_space=pl.ANY)] * 7,
        out_specs=pl.BlockSpec(memory_space=pl.ANY),
        scratch_shapes=[
            big, big, big, pltpu.VMEM((E, G, n), f32), row(3, E), big, big, big,
            pltpu.VMEM(perturbations.shape, jnp.bfloat16), pltpu.VMEM(jacobian.shape, f32),
            pltpu.VMEM((3, rows, n), f32), pltpu.VMEM((rows, n), jnp.int32),
            row(E), row(2, MEM), row(2), row(E), row(2 * H), row(2 * H),
            pltpu.VMEM((rows, G, n), f32),
            dma((5,)), dma((n // 256,)), dma((rows,)), dma((rows,)), dma((6,)), dma((6,)), dma((2,)), dma((2,)), dma((8,)), dma((8,)),
        ],
        compiler_params=pltpu.CompilerParams(
            collective_id=0, has_side_effects=True, vmem_limit_bytes=62 * 1024 * 1024),
    )(controls, perturbations, jacobian, obs_weight, radar_mask, row_faces, col_faces)


def solution(mesh):
    placed = (
        P("mem", "tile", None),
        P("mem", None, "tile", None),
        P(None, "tile", None),
        P("tile", None),
        P("tile", None),
        P("tile", None),
        P("tile", None),
    )
    return jax.shard_map(
        per_device, mesh=mesh, in_specs=placed, out_specs=P("mem", "tile", None), check_vma=False
    )
```

```python
import jax
import jax.numpy as jnp
from jax import lax
from jax.experimental import pallas as pl
from jax.experimental.pallas import tpu as pltpu
from jax.sharding import PartitionSpec as P

MEM = 16
TILE = 32
H = 4
MESH = pl.DeviceIdType.MESH
f32 = jnp.float32
UE = 8


def kernel(ctl, pert, jac, obs, msk, rf, cf, out,
           C, A, B, A2, B2, Q, K, KR, KC, KL, Pv, Jv, nat, natm, part, recv, rown, R, Rup, Rdn, O,
           lsem, psem, csem, osem, hs, hr, fs, fr, ss, sr):
    G = Q.shape[1]
    n = Q.shape[2]
    E = Q.shape[0]
    rows = E - 2 * H
    m = lax.axis_index("mem")
    t = lax.axis_index("tile")
    x = m // 4
    z = m % 4
    has_up = t > 0
    has_dn = t < TILE - 1

    bar = pltpu.get_barrier_semaphore()

    def greet(mm, tt):
        pl.semaphore_signal(bar, inc=1, device_id=(mm, tt), device_id_type=MESH)

    def ring(i, carry):
        greet((m + i) % MEM, t)
        return carry

    def side(tt, full_z, own_z):
        @pl.when(z == full_z)
        def _():
            def body(i, carry):
                greet(i, tt)
                return carry
            lax.fori_loop(0, MEM, body, 0)

        @pl.when(z != full_z)
        def _():
            def body(i, carry):
                greet(i * 4 + own_z, tt)
                return carry
            lax.fori_loop(0, 4, body, 0)

            @pl.when(z != own_z)
            def _():
                greet(m, tt)

    step_cols = 256
    parts = n // step_cols
    small = [
        pltpu.make_async_copy(rf, nat.at[0], lsem.at[0]),
        pltpu.make_async_copy(cf, nat.at[1], lsem.at[1]),
        pltpu.make_async_copy(obs, nat.at[2], lsem.at[2]),
        pltpu.make_async_copy(msk, natm, lsem.at[3]),
    ]
    jload = pltpu.make_async_copy(jac, Jv, lsem.at[4])

    def pload(i):
        cols = pl.ds(i * step_cols, step_cols)
        return pltpu.make_async_copy(pert.at[:, :, :, cols], Pv.at[:, :, :, cols], psem.at[i])

    def cload(r):
        return pltpu.make_async_copy(ctl.at[:, r, :], C.at[1 + H + r], csem.at[r])

    jload.start()
    for i in range(parts):
        pload(i).start()
    for cp in small:
        cp.start()

    lax.fori_loop(1, MEM, ring, 0)

    @pl.when(has_dn)
    def _():
        side(t + 1, 3, 0)

    @pl.when(has_up)
    def _():
        side(t - 1, 0, 3)

    line = jnp.zeros((1, n), f32)

    @pl.when(jnp.logical_not(has_up))
    def _():
        for e in range(H):
            Q[e] = jnp.zeros((G, n), f32)
            for i in range(3):
                K[i, e] = line
        for e in range(2 * H):
            Rup[e] = line

    @pl.when(jnp.logical_not(has_dn))
    def _():
        for e in range(H + rows, E):
            Q[e] = jnp.zeros((G, n), f32)
            for i in range(3):
                K[i, e] = line
        for e in range(2 * H):
            Rdn[e] = line

    for cp in small:
        cp.wait()
    last = jnp.where(has_dn, 1.0, 0.0).astype(f32)
    lane = lax.broadcasted_iota(jnp.int32, (1, n), 1)
    for r in range(rows):
        row = nat[0, r:r + 1, :]
        K[0, H + r] = row * last if r == rows - 1 else row
        K[1, H + r] = jnp.where(lane < n - 1, nat[1, r:r + 1, :], 0.0)
        K[2, H + r] = nat[2, r:r + 1, :] * natm[r:r + 1, :].astype(f32)

    def qtile(j, carry):
        cols = pl.ds(pl.multiple_of(j * 128, 128), 128)
        q = Pv[:, 0, :, cols].astype(f32) * Jv[0, :, cols][None]
        for v in range(1, 4):
            q = q + Pv[:, v, :, cols].astype(f32) * Jv[v, :, cols][None]
        Q[H:H + rows, :, cols] = jnp.swapaxes(q, 0, 1)
        return carry

    jload.wait()
    for i in range(parts):
        pload(i).wait()
        lax.fori_loop(i * step_cols // 128, (i + 1) * step_cols // 128, qtile, 0)
    for r in range(rows):
        cload(r).start()

    near = jnp.where(z == 0, 16, jnp.where(z == 3, 4, 5))
    far = jnp.where(z == 3, 16, jnp.where(z == 0, 4, 5))
    pl.semaphore_wait(bar, MEM - 1 + jnp.where(has_up, near, 0) + jnp.where(has_dn, far, 0))

    def near_copy(src, dst, up, i):
        return pltpu.make_async_remote_copy(
            src, dst, hs.at[i], hr.at[i], device_id=(m, t - 1 if up else t + 1), device_id_type=MESH)

    def halo(up, half):
        k = half * (H // 2)
        return near_copy(
            Q.at[pl.ds((H if up else rows) + k, H // 2)], Q.at[pl.ds((H + rows if up else 0) + k, H // 2)],
            up, (2 if up else 4) + half)

    def piece(up):
        return near_copy(
            K.at[:, pl.ds((H if up else rows) + x, 1)], K.at[:, pl.ds((H + rows if up else 0) + x, 1)],
            up, 0 if up else 1)

    def hand_on(below, i):
        row = K.at[:, pl.ds((H + rows if below else 0) + x, 1)]
        k = 0 if below else 1
        return pltpu.make_async_remote_copy(
            row, row, fs.at[k], fr.at[k], device_id=(((x + i) % 4) * 4 + z, t), device_id_type=MESH)

    def handed(below):
        k = 0 if below else 1
        ref = K.at[:, pl.ds(0, 3)]
        return pltpu.make_async_remote_copy(
            ref, ref, fs.at[k], fr.at[k], device_id=(((x + 1) % 4) * 4 + z, t), device_id_type=MESH)

    @pl.when(has_up)
    def _():
        piece(True).start()

    @pl.when(has_dn)
    def _():
        piece(False).start()

    def send_half(half):
        @pl.when(has_up)
        def _():
            halo(True, half).start()

        @pl.when(has_dn)
        def _():
            halo(False, half).start()

    send_half(0)

    zero = jnp.zeros((G, n), f32)
    for e in list(range(0, H + 1)) + list(range(H + rows + 1, E + 2)):
        C[e] = zero
        A[e] = zero
        B[e] = zero
        A2[e] = zero
        B2[e] = zero
    for e in (0, E + 1):
        KR[e] = zero
        KC[e] = zero
        KL[e] = zero
    def widen(e, carry):
        KR[1 + e] = jnp.broadcast_to(K[0, e], (G, n))
        KC[1 + e] = jnp.broadcast_to(K[1, e], (G, n))
        KL[1 + e] = jnp.broadcast_to(pltpu.roll(K[1, e], 1, 1), (G, n))
        return carry

    lax.fori_loop(H, H + rows, widen, 0)
    def stencil(src, e, count):
        outs = []
        v = src[1 + e]
        up = KR[e] * (v - src[e])
        for i in range(count):
            nxt = src[2 + e + i]
            down = KR[1 + e + i] * (nxt - v)
            flux = KC[1 + e + i] * (pltpu.roll(v, n - 1, 1) - v)
            back = KL[1 + e + i] * (v - pltpu.roll(v, 1, 1))
            outs.append((v + (down - up)) + (flux - back))
            v, up = nxt, down
        return outs

    def step(src, dst, lo, hi, group):
        def body(i, carry):
            e = lo + i * group
            for k, o in enumerate(stencil(src, e, group)):
                dst[1 + e + k] = o
            return carry
        lax.fori_loop(0, (hi - lo) // group, body, 0)

    for r in range(rows):
        cload(r).wait()

    step(C, A, H + 1, H + rows - 1, 7)
    step(A, B, H + 2, H + rows - 2, 6)
    step(B, A2, H + 3, H + rows - 3, 10)
    step(A2, B2, H + 4, H + rows - 4, 8)

    @pl.when(has_up)
    def _():
        piece(False).wait_recv()
        for i in range(1, 4):
            hand_on(False, i).start()

    @pl.when(has_dn)
    def _():
        piece(True).wait_recv()
        for i in range(1, 4):
            hand_on(True, i).start()

    send_half(1)

    @pl.when(has_up)
    def _():
        handed(False).wait_recv()

    @pl.when(has_dn)
    def _():
        handed(True).wait_recv()

    lax.fori_loop(0, H, widen, 0)
    lax.fori_loop(H + rows, E, widen, 0)

    def edges(src, dst, width):
        for lo in (H - width, H + rows - width):
            for k, o in enumerate(stencil(src, lo, 2 * width)):
                dst[1 + lo + k] = o

    edges(C, A, 1)
    edges(A, B, 2)
    edges(B, A2, 3)
    edges(A2, B2, 4)

    def product(e, carry):
        part[e] = jnp.sum(B2[1 + e] * Q[e], axis=0, keepdims=True)
        return carry

    lax.fori_loop(H, H + rows, product, 0)

    peer = (m + 1) % MEM

    def to(src, dst, sem, mm, tt):
        return pltpu.make_async_remote_copy(
            src, dst, ss.at[sem], sr.at[sem], device_id=(mm, tt), device_id_type=MESH)

    def waiter(ref, sem):
        return to(ref, ref, sem, peer, t)

    mine = H + 4 * z + x
    late = jnp.where(z == 0, x, H + rows + x)
    owner_late = jnp.logical_or(z == 0, z == 3)

    def scatter(i, carry):
        o = (m + i) % MEM
        to(part.at[pl.ds(H + 4 * (o % 4) + o // 4, 1)], recv.at[0, pl.ds(m, 1)], 0, o, t).start()
        return carry

    lax.fori_loop(1, MEM, scatter, 0)

    @pl.when(has_up)
    def _():
        halo(False, 0).wait_recv()
        halo(False, 1).wait_recv()

    @pl.when(has_dn)
    def _():
        halo(True, 0).wait_recv()
        halo(True, 1).wait_recv()

    lax.fori_loop(0, H, product, 0)
    lax.fori_loop(H + rows, E, product, 0)

    def scatter_late(i, carry):
        xx = (x + 3 - i) % 4
        for zz, start in ((0, 0), (3, H + rows)):
            @pl.when(jnp.logical_or(xx != x, z != zz))
            def _():
                to(part.at[pl.ds(start + xx, 1)], recv.at[1, pl.ds(m, 1)], 1, xx * 4 + zz, t).start()
        return carry

    lax.fori_loop(0, 4, scatter_late, 0)

    def total(k, row):
        recv[k, pl.ds(m, 1)] = part[pl.ds(row, 1)]
        waiter(recv.at[k, pl.ds(0, MEM - 1)], k).wait_recv()
        sums = [recv[k, i:i + 1] for i in range(MEM)]
        while len(sums) > 1:
            sums = [a + b for a, b in zip(sums[::2], sums[1::2])]
        rown[k:k + 1] = sums[0]
        R[pl.ds(row, 1)] = sums[0]

    def gather(k, row):
        src = rown.at[pl.ds(k, 1)]

        def cross(i, carry, dst, at, sem, tt):
            to(src, dst.at[pl.ds(at, 1)], sem, (m + i) % MEM, tt).start()
            return carry

        @pl.when(jnp.logical_and(z == 0, has_up))
        def _():
            lax.fori_loop(0, MEM, lambda i, c: cross(i, c, Rdn, row, 4 + k, t - 1), 0)

        @pl.when(jnp.logical_and(z == 3, has_dn))
        def _():
            lax.fori_loop(0, MEM, lambda i, c: cross(i, c, Rup, row - rows, 6 + k, t + 1), 0)

        def own(i, carry):
            to(src, R.at[pl.ds(row, 1)], 2 + k, (m + i) % MEM, t).start()
            return carry

        lax.fori_loop(1, MEM, own, 0)

    total(0, mine)
    gather(0, mine)

    @pl.when(owner_late)
    def _():
        total(1, late)
        gather(1, late)

    waiter(R.at[pl.ds(0, MEM - 1)], 2).wait_recv()

    def spread(e, extra):
        r = R[e]
        if extra is not None:
            r = r + extra
        A[1 + e] = Q[e] * jnp.broadcast_to(K[2, e] * r, (G, n))

    def spread_up(e, carry):
        spread(e, Rup[e])
        return carry

    def spread_mid(e, carry):
        spread(e, None)
        return carry

    def spread_dn(e, carry):
        spread(e, Rdn[e - rows])
        return carry

    lax.fori_loop(2 * H, rows, spread_mid, 0)
    step(A, B, 2 * H + 1, rows - 1, 6)
    step(B, A2, 2 * H + 2, rows - 2, 4)
    step(A2, B2, 2 * H + 3, rows - 3, 2)

    @pl.when(has_up)
    def _():
        waiter(Rup.at[pl.ds(0, H)], 6).wait_recv()

    @pl.when(has_dn)
    def _():
        waiter(Rdn.at[pl.ds(0, H)], 4).wait_recv()

    @pl.when(owner_late)
    def _():
        waiter(R.at[pl.ds(0, 2 * H - 1)], 3).wait_recv()

    @pl.when(jnp.logical_not(owner_late))
    def _():
        waiter(R.at[pl.ds(0, 2 * H)], 3).wait_recv()

    @pl.when(has_up)
    def _():
        waiter(Rup.at[pl.ds(0, H)], 7).wait_recv()

    @pl.when(has_dn)
    def _():
        waiter(Rdn.at[pl.ds(0, H)], 5).wait_recv()

    lax.fori_loop(0, 2 * H, spread_up, 0)
    lax.fori_loop(rows, E, spread_dn, 0)
    def rims(src, dst, s):
        for lo in (s, rows - s):
            for k, o in enumerate(stencil(src, lo, 2 * H)):
                dst[1 + lo + k] = o

    rims(A, B, 1)
    rims(B, A2, 2)
    rims(A2, B2, 3)

    def store(r):
        return pltpu.make_async_copy(O.at[r], out.at[:, r, :], osem.at[r])

    for r in range(0, rows, UE):
        for k, o in enumerate(stencil(B2, H + r, UE)):
            O[r + k] = C[1 + H + r + k] + o
            store(r + k).start()

    @pl.when(has_up)
    def _():
        piece(True).wait_send()
        halo(True, 0).wait_send()
        halo(True, 1).wait_send()
        handed(False).wait_send()

    @pl.when(has_dn)
    def _():
        piece(False).wait_send()
        halo(False, 0).wait_send()
        halo(False, 1).wait_send()
        handed(True).wait_send()

    waiter(R.at[pl.ds(0, MEM - 1)], 0).wait_send()
    waiter(R.at[pl.ds(0, MEM - 1)], 2).wait_send()

    @pl.when(owner_late)
    def _():
        waiter(R.at[pl.ds(0, 2 * H - 1)], 1).wait_send()
        waiter(R.at[pl.ds(0, MEM - 1)], 3).wait_send()

    @pl.when(jnp.logical_not(owner_late))
    def _():
        waiter(R.at[pl.ds(0, 2 * H)], 1).wait_send()

    for zz, near, k in ((0, has_up, 4), (3, has_dn, 6)):
        @pl.when(jnp.logical_and(z == zz, near))
        def _():
            waiter(R.at[pl.ds(0, MEM)], k).wait_send()
            waiter(R.at[pl.ds(0, MEM)], k + 1).wait_send()

    for r in range(rows):
        store(r).wait()


def per_device(controls, perturbations, jacobian, obs_weight, radar_mask, row_faces, col_faces):
    G, rows, n = controls.shape
    E = rows + 2 * H
    big = pltpu.VMEM((E + 2, G, n), f32)
    row = lambda *s: pltpu.VMEM(s + (1, n), f32)
    dma = pltpu.SemaphoreType.DMA
    return pl.pallas_call(
        kernel,
        out_shape=jax.ShapeDtypeStruct(controls.shape, f32),
        in_specs=[pl.BlockSpec(memory_space=pl.ANY)] * 7,
        out_specs=pl.BlockSpec(memory_space=pl.ANY),
        scratch_shapes=[
            big, big, big, big, big, pltpu.VMEM((E, G, n), f32), row(3, E), big, big, big,
            pltpu.VMEM(perturbations.shape, jnp.bfloat16), pltpu.VMEM(jacobian.shape, f32),
            pltpu.VMEM((3, rows, n), f32), pltpu.VMEM((rows, n), jnp.int32),
            row(E), row(2, MEM), row(2), row(E), row(2 * H), row(2 * H),
            pltpu.VMEM((rows, G, n), f32),
            dma((5,)), dma((n // 256,)), dma((rows,)), dma((rows,)), dma((6,)), dma((6,)), dma((2,)), dma((2,)), dma((8,)), dma((8,)),
        ],
        compiler_params=pltpu.CompilerParams(
            collective_id=0, has_side_effects=True, vmem_limit_bytes=62 * 1024 * 1024),
    )(controls, perturbations, jacobian, obs_weight, radar_mask, row_faces, col_faces)


def solution(mesh):
    placed = (
        P("mem", "tile", None),
        P("mem", None, "tile", None),
        P(None, "tile", None),
        P("tile", None),
        P("tile", None),
        P("tile", None),
        P("tile", None),
    )
    return jax.shard_map(
        per_device, mesh=mesh, in_specs=placed, out_specs=P("mem", "tile", None), check_vma=False
    )
```

```python
import jax
import jax.numpy as jnp
from jax import lax
from jax.experimental import pallas as pl
from jax.experimental.pallas import tpu as pltpu
from jax.sharding import PartitionSpec as P

MEM = 16
TILE = 32
H = 4
MESH = pl.DeviceIdType.MESH
f32 = jnp.float32
UE = 8


def kernel(ctl, pert, jac, obs, msk, rf, cf, out,
           C, A, B, A2, B2, Q, K, KR, KC, KL, Pv, Jv, nat, natm, part, recv, rown, R, Rup, Rdn, O,
           lsem, psem, csem, osem, hs, hr, fs, fr, ss, sr):
    G = Q.shape[1]
    n = Q.shape[2]
    E = Q.shape[0]
    rows = E - 2 * H
    m = lax.axis_index("mem")
    t = lax.axis_index("tile")
    x = lax.div(m, 4)
    z = lax.rem(m, 4)
    has_up = t > 0
    has_dn = t < TILE - 1

    bar = pltpu.get_barrier_semaphore()

    def greet(mm, tt):
        pl.semaphore_signal(bar, inc=1, device_id=(mm, tt), device_id_type=MESH)

    def ring(i, carry):
        greet(lax.rem(m + i, MEM), t)
        return carry

    def side(tt, full_z, own_z):
        @pl.when(z == full_z)
        def _():
            def body(i, carry):
                greet(i, tt)
                return carry
            lax.fori_loop(0, MEM, body, 0)

        @pl.when(z != full_z)
        def _():
            def body(i, carry):
                greet(i * 4 + own_z, tt)
                return carry
            lax.fori_loop(0, 4, body, 0)

            @pl.when(z != own_z)
            def _():
                greet(m, tt)

    step_cols = 256
    parts = n // step_cols
    small = [
        pltpu.make_async_copy(rf, nat.at[0], lsem.at[0]),
        pltpu.make_async_copy(cf, nat.at[1], lsem.at[1]),
        pltpu.make_async_copy(obs, nat.at[2], lsem.at[2]),
        pltpu.make_async_copy(msk, natm, lsem.at[3]),
    ]
    jload = pltpu.make_async_copy(jac, Jv, lsem.at[4])

    def pload(i):
        cols = pl.ds(i * step_cols, step_cols)
        return pltpu.make_async_copy(pert.at[:, :, :, cols], Pv.at[:, :, :, cols], psem.at[i])

    def cload(r):
        return pltpu.make_async_copy(ctl.at[:, r, :], C.at[1 + H + r], csem.at[r])

    jload.start()
    for i in range(parts):
        pload(i).start()
    for cp in small:
        cp.start()

    lax.fori_loop(1, MEM, ring, 0)

    @pl.when(has_dn)
    def _():
        side(t + 1, 3, 0)

    @pl.when(has_up)
    def _():
        side(t - 1, 0, 3)

    line = jnp.zeros((1, n), f32)

    @pl.when(jnp.logical_not(has_up))
    def _():
        for e in range(H):
            Q[e] = jnp.zeros((G, n), f32)
            for i in range(3):
                K[i, e] = line
        for e in range(2 * H):
            Rup[e] = line

    @pl.when(jnp.logical_not(has_dn))
    def _():
        for e in range(H + rows, E):
            Q[e] = jnp.zeros((G, n), f32)
            for i in range(3):
                K[i, e] = line
        for e in range(2 * H):
            Rdn[e] = line

    for cp in small:
        cp.wait()
    last = jnp.where(has_dn, 1.0, 0.0).astype(f32)
    lane = lax.broadcasted_iota(jnp.int32, (1, n), 1)
    for r in range(rows):
        row = nat[0, r:r + 1, :]
        K[0, H + r] = row * last if r == rows - 1 else row
        K[1, H + r] = jnp.where(lane < n - 1, nat[1, r:r + 1, :], 0.0)
        K[2, H + r] = nat[2, r:r + 1, :] * natm[r:r + 1, :].astype(f32)

    def qtile(j, carry):
        cols = pl.ds(pl.multiple_of(j * 128, 128), 128)
        q = Pv[:, 0, :, cols].astype(f32) * Jv[0, :, cols][None]
        for v in range(1, 4):
            q = q + Pv[:, v, :, cols].astype(f32) * Jv[v, :, cols][None]
        Q[H:H + rows, :, cols] = jnp.swapaxes(q, 0, 1)
        return carry

    jload.wait()
    for i in range(parts):
        pload(i).wait()
        lax.fori_loop(i * step_cols // 128, (i + 1) * step_cols // 128, qtile, 0)
    for r in range(rows):
        cload(r).start()

    near = jnp.where(z == 0, 16, jnp.where(z == 3, 4, 5))
    far = jnp.where(z == 3, 16, jnp.where(z == 0, 4, 5))
    pl.semaphore_wait(bar, MEM - 1 + jnp.where(has_up, near, 0) + jnp.where(has_dn, far, 0))

    def near_copy(src, dst, up, i):
        return pltpu.make_async_remote_copy(
            src, dst, hs.at[i], hr.at[i], device_id=(m, t - 1 if up else t + 1), device_id_type=MESH)

    def halo(up, half):
        k = half * (H // 2)
        return near_copy(
            Q.at[pl.ds((H if up else rows) + k, H // 2)], Q.at[pl.ds((H + rows if up else 0) + k, H // 2)],
            up, (2 if up else 4) + half)

    def piece(up):
        return near_copy(
            K.at[:, pl.ds((H if up else rows) + x, 1)], K.at[:, pl.ds((H + rows if up else 0) + x, 1)],
            up, 0 if up else 1)

    def hand_on(below, i):
        row = K.at[:, pl.ds((H + rows if below else 0) + x, 1)]
        k = 0 if below else 1
        return pltpu.make_async_remote_copy(
            row, row, fs.at[k], fr.at[k], device_id=(lax.rem(x + i, 4) * 4 + z, t), device_id_type=MESH)

    def handed(below):
        k = 0 if below else 1
        ref = K.at[:, pl.ds(0, 3)]
        return pltpu.make_async_remote_copy(
            ref, ref, fs.at[k], fr.at[k], device_id=(((x + 1) % 4) * 4 + z, t), device_id_type=MESH)

    @pl.when(has_up)
    def _():
        piece(True).start()

    @pl.when(has_dn)
    def _():
        piece(False).start()

    def send_half(half):
        @pl.when(has_up)
        def _():
            halo(True, half).start()

        @pl.when(has_dn)
        def _():
            halo(False, half).start()

    send_half(0)

    zero = jnp.zeros((G, n), f32)
    for e in list(range(0, H + 1)) + list(range(H + rows + 1, E + 2)):
        C[e] = zero
        A[e] = zero
        B[e] = zero
        A2[e] = zero
        B2[e] = zero
    for e in (0, E + 1):
        KR[e] = zero
        KC[e] = zero
        KL[e] = zero
    def widen(e, carry):
        KR[1 + e] = jnp.broadcast_to(K[0, e], (G, n))
        KC[1 + e] = jnp.broadcast_to(K[1, e], (G, n))
        KL[1 + e] = jnp.broadcast_to(pltpu.roll(K[1, e], 1, 1), (G, n))
        return carry

    lax.fori_loop(H, H + rows, widen, 0)
    def stencil(src, e, count):
        outs = []
        v = src[1 + e]
        up = KR[e] * (v - src[e])
        for i in range(count):
            nxt = src[2 + e + i]
            down = KR[1 + e + i] * (nxt - v)
            flux = KC[1 + e + i] * (pltpu.roll(v, n - 1, 1) - v)
            back = KL[1 + e + i] * (v - pltpu.roll(v, 1, 1))
            outs.append((v + (down - up)) + (flux - back))
            v, up = nxt, down
        return outs

    def step(src, dst, lo, hi, group):
        def body(i, carry):
            e = lo + i * group
            for k, o in enumerate(stencil(src, e, group)):
                dst[1 + e + k] = o
            return carry
        lax.fori_loop(0, (hi - lo) // group, body, 0)

    for r in range(rows):
        cload(r).wait()

    step(C, A, H + 1, H + rows - 1, 7)
    step(A, B, H + 2, H + rows - 2, 6)
    step(B, A2, H + 3, H + rows - 3, 10)
    step(A2, B2, H + 4, H + rows - 4, 8)

    @pl.when(has_up)
    def _():
        piece(False).wait_recv()
        for i in range(1, 4):
            hand_on(False, i).start()

    @pl.when(has_dn)
    def _():
        piece(True).wait_recv()
        for i in range(1, 4):
            hand_on(True, i).start()

    send_half(1)

    @pl.when(has_up)
    def _():
        handed(False).wait_recv()

    @pl.when(has_dn)
    def _():
        handed(True).wait_recv()

    lax.fori_loop(0, H, widen, 0)
    lax.fori_loop(H + rows, E, widen, 0)

    def edges(src, dst, width):
        for lo in (H - width, H + rows - width):
            for k, o in enumerate(stencil(src, lo, 2 * width)):
                dst[1 + lo + k] = o

    edges(C, A, 1)
    edges(A, B, 2)
    edges(B, A2, 3)
    edges(A2, B2, 4)

    def product(e, carry):
        part[e] = jnp.sum(B2[1 + e] * Q[e], axis=0, keepdims=True)
        return carry

    lax.fori_loop(H, H + rows, product, 0)

    peer = (m + 1) % MEM

    def to(src, dst, sem, mm, tt):
        return pltpu.make_async_remote_copy(
            src, dst, ss.at[sem], sr.at[sem], device_id=(mm, tt), device_id_type=MESH)

    def waiter(ref, sem):
        return to(ref, ref, sem, peer, t)

    mine = H + 4 * z + x
    late = jnp.where(z == 0, x, H + rows + x)
    owner_late = jnp.logical_or(z == 0, z == 3)

    def scatter(i, carry):
        o = lax.rem(m + i, MEM)
        to(part.at[pl.ds(H + 4 * lax.rem(o, 4) + lax.div(o, 4), 1)], recv.at[0, pl.ds(m, 1)], 0, o, t).start()
        return carry

    lax.fori_loop(1, MEM, scatter, 0)

    @pl.when(has_up)
    def _():
        halo(False, 0).wait_recv()
        halo(False, 1).wait_recv()

    @pl.when(has_dn)
    def _():
        halo(True, 0).wait_recv()
        halo(True, 1).wait_recv()

    lax.fori_loop(0, H, product, 0)
    lax.fori_loop(H + rows, E, product, 0)

    def scatter_late(i, carry):
        xx = lax.rem(x + 3 - i + 4, 4)
        for zz, start in ((0, 0), (3, H + rows)):
            @pl.when(jnp.logical_or(xx != x, z != zz))
            def _():
                to(part.at[pl.ds(start + xx, 1)], recv.at[1, pl.ds(m, 1)], 1, xx * 4 + zz, t).start()
        return carry

    lax.fori_loop(0, 4, scatter_late, 0)

    def total(k, row):
        recv[k, pl.ds(m, 1)] = part[pl.ds(row, 1)]
        waiter(recv.at[k, pl.ds(0, MEM - 1)], k).wait_recv()
        sums = [recv[k, i:i + 1] for i in range(MEM)]
        while len(sums) > 1:
            sums = [a + b for a, b in zip(sums[::2], sums[1::2])]
        rown[k:k + 1] = sums[0]
        R[pl.ds(row, 1)] = sums[0]

    def gather(k, row):
        src = rown.at[pl.ds(k, 1)]

        def cross(i, carry, dst, at, sem, tt):
            to(src, dst.at[pl.ds(at, 1)], sem, lax.rem(m + i, MEM), tt).start()
            return carry

        @pl.when(jnp.logical_and(z == 0, has_up))
        def _():
            lax.fori_loop(0, MEM, lambda i, c: cross(i, c, Rdn, row, 4 + k, t - 1), 0)

        @pl.when(jnp.logical_and(z == 3, has_dn))
        def _():
            lax.fori_loop(0, MEM, lambda i, c: cross(i, c, Rup, row - rows, 6 + k, t + 1), 0)

        def own(i, carry):
            to(src, R.at[pl.ds(row, 1)], 2 + k, lax.rem(m + i, MEM), t).start()
            return carry

        lax.fori_loop(1, MEM, own, 0)

    total(0, mine)
    gather(0, mine)

    @pl.when(owner_late)
    def _():
        total(1, late)
        gather(1, late)

    waiter(R.at[pl.ds(0, MEM - 1)], 2).wait_recv()

    def spread(e, extra):
        r = R[e]
        if extra is not None:
            r = r + extra
        A[1 + e] = Q[e] * jnp.broadcast_to(K[2, e] * r, (G, n))

    def spread_up(e, carry):
        spread(e, Rup[e])
        return carry

    def spread_mid(e, carry):
        spread(e, None)
        return carry

    def spread_dn(e, carry):
        spread(e, Rdn[e - rows])
        return carry

    lax.fori_loop(2 * H, rows, spread_mid, 0)
    step(A, B, 2 * H + 1, rows - 1, 6)
    step(B, A2, 2 * H + 2, rows - 2, 4)
    step(A2, B2, 2 * H + 3, rows - 3, 2)

    @pl.when(has_up)
    def _():
        waiter(Rup.at[pl.ds(0, H)], 6).wait_recv()

    @pl.when(has_dn)
    def _():
        waiter(Rdn.at[pl.ds(0, H)], 4).wait_recv()

    @pl.when(owner_late)
    def _():
        waiter(R.at[pl.ds(0, 2 * H - 1)], 3).wait_recv()

    @pl.when(jnp.logical_not(owner_late))
    def _():
        waiter(R.at[pl.ds(0, 2 * H)], 3).wait_recv()

    @pl.when(has_up)
    def _():
        waiter(Rup.at[pl.ds(0, H)], 7).wait_recv()

    @pl.when(has_dn)
    def _():
        waiter(Rdn.at[pl.ds(0, H)], 5).wait_recv()

    lax.fori_loop(0, 2 * H, spread_up, 0)
    lax.fori_loop(rows, E, spread_dn, 0)
    def rims(src, dst, s):
        for lo in (s, rows - s):
            for k, o in enumerate(stencil(src, lo, 2 * H)):
                dst[1 + lo + k] = o

    rims(A, B, 1)
    rims(B, A2, 2)
    rims(A2, B2, 3)

    def store(r):
        return pltpu.make_async_copy(O.at[r], out.at[:, r, :], osem.at[r])

    for r in range(0, rows, UE):
        for k, o in enumerate(stencil(B2, H + r, UE)):
            O[r + k] = C[1 + H + r + k] + o
            store(r + k).start()

    @pl.when(has_up)
    def _():
        piece(True).wait_send()
        halo(True, 0).wait_send()
        halo(True, 1).wait_send()
        handed(False).wait_send()

    @pl.when(has_dn)
    def _():
        piece(False).wait_send()
        halo(False, 0).wait_send()
        halo(False, 1).wait_send()
        handed(True).wait_send()

    waiter(R.at[pl.ds(0, MEM - 1)], 0).wait_send()
    waiter(R.at[pl.ds(0, MEM - 1)], 2).wait_send()

    @pl.when(owner_late)
    def _():
        waiter(R.at[pl.ds(0, 2 * H - 1)], 1).wait_send()
        waiter(R.at[pl.ds(0, MEM - 1)], 3).wait_send()

    @pl.when(jnp.logical_not(owner_late))
    def _():
        waiter(R.at[pl.ds(0, 2 * H)], 1).wait_send()

    for zz, near, k in ((0, has_up, 4), (3, has_dn, 6)):
        @pl.when(jnp.logical_and(z == zz, near))
        def _():
            waiter(R.at[pl.ds(0, MEM)], k).wait_send()
            waiter(R.at[pl.ds(0, MEM)], k + 1).wait_send()

    for r in range(rows):
        store(r).wait()


def per_device(controls, perturbations, jacobian, obs_weight, radar_mask, row_faces, col_faces):
    G, rows, n = controls.shape
    E = rows + 2 * H
    big = pltpu.VMEM((E + 2, G, n), f32)
    row = lambda *s: pltpu.VMEM(s + (1, n), f32)
    dma = pltpu.SemaphoreType.DMA
    return pl.pallas_call(
        kernel,
        out_shape=jax.ShapeDtypeStruct(controls.shape, f32),
        in_specs=[pl.BlockSpec(memory_space=pl.ANY)] * 7,
        out_specs=pl.BlockSpec(memory_space=pl.ANY),
        scratch_shapes=[
            big, big, big, big, big, pltpu.VMEM((E, G, n), f32), row(3, E), big, big, big,
            pltpu.VMEM(perturbations.shape, jnp.bfloat16), pltpu.VMEM(jacobian.shape, f32),
            pltpu.VMEM((3, rows, n), f32), pltpu.VMEM((rows, n), jnp.int32),
            row(E), row(2, MEM), row(2), row(E), row(2 * H), row(2 * H),
            pltpu.VMEM((rows, G, n), f32),
            dma((5,)), dma((n // 256,)), dma((rows,)), dma((rows,)), dma((6,)), dma((6,)), dma((2,)), dma((2,)), dma((8,)), dma((8,)),
        ],
        compiler_params=pltpu.CompilerParams(
            collective_id=0, has_side_effects=True, vmem_limit_bytes=62 * 1024 * 1024),
    )(controls, perturbations, jacobian, obs_weight, radar_mask, row_faces, col_faces)


def solution(mesh):
    placed = (
        P("mem", "tile", None),
        P("mem", None, "tile", None),
        P(None, "tile", None),
        P("tile", None),
        P("tile", None),
        P("tile", None),
        P("tile", None),
    )
    return jax.shard_map(
        per_device, mesh=mesh, in_specs=placed, out_specs=P("mem", "tile", None), check_vma=False
    )
```
